128 devices in a mesh: tm: 32 (over x, z_hi, y), space: 4 (over z_lo, core).
Axes of the slice: x: 4, y: 4, z: 4 (z_hi: 2, z_lo: 2; z = z_hi * 2 + z_lo), core: 2. Of those that a mesh axis runs over, the one named last changes fastest.
Arguments:
- snapshots: bfloat16 [8192, 32768], P('space', 'tm'), may hold values from -6 to 6
Outputs:
- hankel: float32 [32768, 5, 1024], P(('tm', 'space'))
The draws below stay inside these ranges and needn't reach their ends.
All inputs are finite; a program needn't handle non-finite values.
Results may differ from the reference program's by a relative error of at most 0.0003.
Values may be sent and summed in bfloat16 or wider, within the bound.
A program may use at most 128 MiB of HBM per device.

```python
import math
import jax
import jax.numpy as jnp
from jax import lax

B = 1024
DELAY = 8
PAIRS = 5
CELLS = 8192
SNAPS = 32768


def levels(stream_key, dims, cuts, least, top_value):
    def one(position, shards_of):
        steps = jax.random.uniform(jax.random.fold_in(jax.random.fold_in(stream_key, 6), position), (shards_of,), jnp.float32, least / len(cuts), top_value / len(cuts))
        return jnp.repeat(jnp.exp(steps), dims[position] // shards_of).reshape((-1,) + (1,) * (len(dims) - position - 1))

    loudness = one(*cuts[0])
    for cut in cuts[1:]:
        loudness = loudness * one(*cut)
    return loudness


def normal_values(rng, dims, spread, reach, split=(), kind=jnp.bfloat16):
    values = spread * jax.random.normal(rng, dims, jnp.float32)
    if split:
        values = values * levels(rng, dims, split, -0.22, 0.18)
    return jnp.clip(values, -reach, reach).astype(kind)


def setup_inputs(seed: int = 0) -> dict:
    seeds = jax.random.split(jax.random.key(seed), 2)
    snapshots = normal_values(seeds[0], (CELLS, SNAPS), 1.0, 6.0, ((0, 4), (1, 32)))
    return {"snapshots": snapshots}


def window_sum(gram):
    total = jnp.zeros((B, B), jnp.float32)
    for shift_k in range(DELAY):
        total = total + gram[shift_k:shift_k + B, shift_k:shift_k + B]
    return total

def reference(snapshots):
    blocks = SNAPS // B
    padded = jnp.concatenate([snapshots, jnp.zeros((CELLS, DELAY - 1), jnp.bfloat16)], axis=1)
    scale_factor = 1.0 / math.sqrt(DELAY * CELLS)

    def row_block(block_a):
        left = lax.dynamic_slice_in_dim(padded, (block_a * B).astype(jnp.int32), B + DELAY - 1, 1)
        tiles = []
        for offset in range(PAIRS):
            block_b = ((block_a - offset) % blocks).astype(jnp.int32)
            right = lax.dynamic_slice_in_dim(padded, block_b * B, B + DELAY - 1, 1)
            gram = lax.dot_general(left, right, (((0,), (0,)), ((), ())), preferred_element_type=jnp.float32)
            tiles.append(window_sum(gram) * scale_factor)
        return jnp.stack(tiles, axis=1)
    result = lax.map(row_block, jnp.arange(blocks, dtype=jnp.int32))
    return result.reshape(SNAPS, PAIRS, B)
```

```python
import functools
import math

import jax
import jax.numpy as jnp
from jax import lax
from jax.experimental import pallas as pl
from jax.experimental.pallas import tpu as pltpu
from jax.sharding import PartitionSpec as P

DELAY = 8
PAIRS = 5
CHUNKS = 4
HEAD = 16
POWER = 14.0
TOP = 125.0 * math.log(2.0)
MESH = pl.DeviceIdType.MESH
ORDER = [
    (4, 0), (1, 0), (3, 0), (0, 0), 4,
    (4, 1), (1, 1), (0, 1), (3, 1), 5,
    (0, 2), (0, 3), (4, 2), 6,
    (1, 2), (3, 2), 7,
    (4, 3), (1, 3), (2, 0), (2, 1), (2, 2), (3, 3), (2, 3),
]
TASKS = [entry for entry in ORDER if isinstance(entry, tuple)]
STAGES = 3


def encode(value):
    top = jnp.max(jnp.abs(value), axis=0, keepdims=True)
    top = jnp.maximum(top, 1e-35).astype(jnp.bfloat16)
    ratio = jnp.abs(value) / top.astype(jnp.float32)
    code = jnp.exp(POWER * jnp.log(jnp.maximum(ratio, 1e-30)) + TOP)
    code = jnp.where(value < 0.0, -code, code).astype(jnp.bfloat16)
    return code, jnp.broadcast_to(top, (HEAD, value.shape[1]))


def decode(code, top):
    code = code.astype(jnp.float32)
    size = jnp.exp((jnp.log(jnp.maximum(jnp.abs(code), 1e-37)) - TOP) * (1.0 / POWER))
    size = size * top.astype(jnp.float32)
    return jnp.where(code == 0.0, 0.0, jnp.where(code < 0.0, -size, size))


def kernel(
    count, scale, x_ref, out_ref,
    buf, at, hb, hx, hn, halo, stage, inbox, zout, zin, acc, rout, rin,
    local_sem, swap_s, swap_r, cross_s, cross_r, plus_s, plus_r, minus_s, minus_r,
    hswap_s, hswap_r, head_s, head_r, core_s, core_r, z_s, z_r, back_s, back_r, out_sem,
):
    cells, width = x_ref.shape
    half = cells // 2
    chunk = width // CHUNKS
    strip = width // 4
    rows = strip + HEAD
    lane = halo.shape[-1]

    t = lax.axis_index("tm")
    s = lax.axis_index("space")
    y = lax.rem(t, 4)
    base = t - y
    zh = lax.rem(lax.div(t, 4), 2)
    zlo = lax.div(s, 2)
    core = lax.rem(s, 2)
    flip = (1 - zlo) * 2 + core
    keep = pl.multiple_of(zh * half, half)
    away = pl.multiple_of((1 - zh) * half, half)

    def block(steps):
        return lax.rem(t + steps + count, count)

    def aligned(steps):
        there = block(steps)
        other = lax.rem(lax.div(there, 4), 2)
        return there, lax.select(other == zh, s, flip)

    partner = (t, flip)
    sibling = (t, zlo * 2 + 1 - core)
    above = (base + lax.rem(y + 1, 4), s)
    below = (base + lax.rem(y + 3, 4), s)
    onward = (block(4), flip)
    heads_to = [aligned(-1), aligned(2), aligned(3)]
    home = (block(-1), s)

    barrier = pltpu.get_barrier_semaphore()
    greet = [partner, sibling, above, below, onward, (block(-4), flip)]
    greet += heads_to + [aligned(1), aligned(-2), aligned(-3)]
    greet += [home, (block(1), s)]
    for device in greet:
        pl.semaphore_signal(barrier, inc=1, device_id=device, device_id_type=MESH)
    pl.semaphore_wait(barrier, len(greet))

    def remote(src, dst, send, recv, device):
        return pltpu.make_async_remote_copy(
            src_ref=src, dst_ref=dst, send_sem=send, recv_sem=recv,
            device_id=device, device_id_type=MESH,
        )

    def local(n):
        q = CHUNKS - 1 - n
        return pltpu.make_async_copy(
            x_ref.at[pl.ds(keep, half), q * chunk : (q + 1) * chunk],
            buf.at[0, q, pl.ds(keep, half), :],
            local_sem.at[n],
        )

    def swap(n):
        q = CHUNKS - 1 - n
        return remote(
            x_ref.at[pl.ds(away, half), q * chunk : (q + 1) * chunk],
            buf.at[0, q, pl.ds(away, half), :],
            swap_s.at[n], swap_r.at[n], partner,
        )

    def stream(n, phase, source, target, off, send, recv, device):
        q = CHUNKS - 1 - n
        return remote(
            buf.at[source, q, pl.ds(off, half), :],
            buf.at[target, q, pl.ds(off, half), :],
            send.at[n, phase], recv.at[n, phase], device,
        )

    def cross(n, phase):
        off = keep if phase == 0 else away
        return stream(n, phase, 0, 3, off, cross_s, cross_r, onward)

    def plus(n, phase, source, off):
        return stream(n, phase, source, 1, off, plus_s, plus_r, above)

    def minus(n, phase, source, off):
        return stream(n, phase, source, 2, off, minus_s, minus_r, below)

    def own_ready(n, phase):
        off = keep if phase == 0 else away
        cross(n, phase).start()

        @pl.when(y < 3)
        def _():
            plus(n, phase, 0, off).start()

        @pl.when(y == 0)
        def _():
            minus(n, phase, 0, off).start()

    def cross_ready(index):
        n, phase = index // 2, index % 2
        off = away if phase == 0 else keep
        cross(n, phase).wait_recv()

        @pl.when(y == 3)
        def _():
            plus(n, phase, 3, off).start()

        @pl.when(y > 0)
        def _():
            minus(n, phase, 3, off).start()

    def transpose(which, source, n):
        q = CHUNKS - 1 - n

        @pl.loop(0, cells // strip)
        def _(i):
            at_cell = pl.multiple_of(i * strip, strip)
            at[which, q * chunk : (q + 1) * chunk, pl.ds(at_cell, strip)] = buf[
                source, q, pl.ds(at_cell, strip), :
            ].T

    head_copy = pltpu.make_async_copy(x_ref.at[:, 0:lane], hx, local_sem.at[CHUNKS])
    head_copy.start()
    for n in range(CHUNKS):
        local(n).start()
    for n in range(CHUNKS):
        swap(n).start()

    local(0).wait()
    own_ready(0, 0)

    head_copy.wait()

    @pl.loop(0, cells // strip)
    def _(i):
        at_cell = pl.multiple_of(i * strip, strip)
        piece = hx[pl.ds(at_cell, strip), :].T[0:HEAD]
        hn[:, pl.ds(at_cell, strip)] = jnp.where(t == 0, jnp.zeros_like(piece), piece)

    hb[1, :, pl.ds(keep, half)] = hn[:, pl.ds(keep, half)]
    head_swap = remote(
        hn.at[:, pl.ds(away, half)], hb.at[1, :, pl.ds(away, half)],
        hswap_s, hswap_r, partner,
    )
    head_swap.start()
    head_swap.wait_recv()
    heads = [
        remote(hb.at[1], hb.at[slot], head_s.at[i], head_r.at[i], device)
        for i, (slot, device) in enumerate(zip((0, 2, 3), heads_to))
    ]
    for copy in heads:
        copy.start()
    at[1, width : width + HEAD, :] = hb[1]

    for n in range(CHUNKS):
        swap(n).wait_recv()
        own_ready(n, 1)
        if n + 1 < CHUNKS:
            local(n + 1).wait()
            own_ready(n + 1, 0)
        if n == 0:
            for copy in heads:
                copy.wait_recv()
            at[0, width : width + HEAD, :] = hb[0]
        transpose(0, 0, n)
        cross_ready(n)

    def core_copy(k):
        return remote(
            stage.at[k % STAGES, 1 - core], inbox.at[k],
            core_s.at[k], core_r.at[k], sibling,
        )

    def z_copy(k):
        return remote(zout.at[k], zin.at[k], z_s.at[k], z_r.at[k], partner)

    def back_copy(n):
        return remote(rout.at[n], rin.at[n], back_s.at[n], back_r.at[n], home)

    def out_copy(k):
        r, n = TASKS[k]
        q = CHUNKS - 1 - n
        return pltpu.make_async_copy(
            acc.at[k], out_ref.at[r, :, q * chunk : (q + 1) * chunk], out_sem.at[k]
        )

    def compute(k):
        r, n = TASKS[k]
        q = CHUNKS - 1 - n
        left = 1 if r == 2 else 0
        right = (0, 1, 2, 2, 3)[r]
        if k >= STAGES:
            core_copy(k - STAGES).wait_send()

        @pl.loop(0, 4)
        def _(p):
            lhs = at[left, pl.ds(pl.multiple_of(p * strip, strip), rows), :]
            gram = jnp.dot(lhs, buf[right, q], preferred_element_type=jnp.float32)
            if n == 0:
                after = lax.dot_general(
                    lhs, hb[right], (((1,), (1,)), ((), ())),
                    preferred_element_type=jnp.float32,
                )
                halo[r, p, :, 0:HEAD] = after
            full = jnp.concatenate([gram, halo[r, p]], axis=1)
            halo[r, p] = gram[:, 0:lane]
            by = 1
            while by < DELAY:
                moved = pltpu.roll(full, rows - by, 0)
                full = full + pltpu.roll(moved, chunk + lane - by, 1)
                by *= 2
            stage[k % STAGES, lax.rem(p, 2), lax.div(p, 2)] = (
                full[0:strip, 0:chunk] * scale
            )

        core_copy(k).start()

    def send_z(k):
        core_copy(k).wait_recv()
        slot = k % STAGES
        acc[k] = stage[slot, core, zlo] + inbox[k, zlo]
        code, top = encode(stage[slot, core, 1 - zlo] + inbox[k, 1 - zlo])
        zout[k, 0:strip] = code
        zout[k, strip:rows] = top
        z_copy(k).start()

    def finish(k):
        r, n = TASKS[k]
        z_copy(k).wait_recv()
        total = acc[k] + decode(zin[k, 0:strip], zin[k, strip : strip + 1])
        if r == 2:
            code, top = encode(total)
            rout[n, 0:strip] = code
            rout[n, strip:rows] = top
            back_copy(n).start()
        else:
            acc[k] = total
            out_copy(k).start()

    def block_ready(n, kind):
        for phase in range(2):
            kind(n, phase, 0, keep).wait_recv()

    k = 0
    for entry in ORDER:
        if not isinstance(entry, tuple):
            cross_ready(entry)
            continue
        r, n = entry
        if r == 1:
            block_ready(n, plus)
            transpose(1, 1, n)
        if r == 3:
            block_ready(n, minus)
        compute(k)
        if k >= 1:
            send_z(k - 1)
        if k >= 3:
            finish(k - 3)
        k += 1
    send_z(k - 1)
    for j in range(k - 3, k):
        finish(j)
    for j, (r, n) in enumerate(TASKS):
        if r == 2:
            back_copy(n).wait_recv()
            acc[j] = decode(rin[n, 0:strip], rin[n, strip : strip + 1])
            out_copy(j).start()

    for n in range(CHUNKS):
        swap(n).wait_send()
        back_copy(n).wait_send()
        for phase in range(2):
            cross(n, phase).wait_send()
            plus(n, phase, 0, keep).wait_send()
            minus(n, phase, 0, keep).wait_send()
    head_swap.wait_send()
    for copy in heads:
        copy.wait_send()
    for j in range(k):
        if j >= k - STAGES:
            core_copy(j).wait_send()
        z_copy(j).wait_send()
        out_copy(j).wait()


def body(snapshots):
    cells, width = snapshots.shape
    count = lax.axis_size("tm")
    scale = 1.0 / math.sqrt(DELAY * cells * lax.axis_size("space"))
    strip, chunk, half = width // 4, width // CHUNKS, cells // 2
    rows = strip + HEAD
    lane = 128
    tasks = len(TASKS)
    dma = pltpu.SemaphoreType.DMA
    f32, bf16 = jnp.float32, jnp.bfloat16
    out = pl.pallas_call(
        functools.partial(kernel, count, scale),
        out_shape=jax.ShapeDtypeStruct((PAIRS, strip, width), f32),
        in_specs=[pl.BlockSpec(memory_space=pl.ANY)],
        out_specs=pl.BlockSpec(memory_space=pl.ANY),
        scratch_shapes=[
            pltpu.VMEM((4, CHUNKS, cells, chunk), bf16),
            pltpu.VMEM((2, width + HEAD, cells), bf16),
            pltpu.VMEM((4, HEAD, cells), bf16),
            pltpu.VMEM((cells, lane), bf16),
            pltpu.VMEM((HEAD, cells), bf16),
            pltpu.VMEM((PAIRS, 4, rows, lane), f32),
            pltpu.VMEM((STAGES, 2, 2, strip, chunk), f32),
            pltpu.VMEM((tasks, 2, strip, chunk), f32),
            pltpu.VMEM((tasks, rows, chunk), bf16),
            pltpu.VMEM((tasks, rows, chunk), bf16),
            pltpu.VMEM((tasks, strip, chunk), f32),
            pltpu.VMEM((CHUNKS, rows, chunk), bf16),
            pltpu.VMEM((CHUNKS, rows, chunk), bf16),
            dma((CHUNKS + 1,)),
            dma((CHUNKS,)), dma((CHUNKS,)),
            dma((CHUNKS, 2)), dma((CHUNKS, 2)),
            dma((CHUNKS, 2)), dma((CHUNKS, 2)),
            dma((CHUNKS, 2)), dma((CHUNKS, 2)),
            dma, dma,
            dma((3,)), dma((3,)),
            dma((tasks,)), dma((tasks,)),
            dma((tasks,)), dma((tasks,)),
            dma((CHUNKS,)), dma((CHUNKS,)),
            dma((tasks,)),
        ],
        compiler_params=pltpu.CompilerParams(
            collective_id=0, has_side_effects=True, vmem_limit_bytes=60 * 2**20
        ),
        cost_estimate=pl.CostEstimate(
            flops=2 * PAIRS * width * width * cells,
            bytes_accessed=2 * cells * width + 4 * PAIRS * strip * width,
            transcendentals=0,
        ),
    )(snapshots)
    return jnp.transpose(out, (1, 0, 2))


def solution(mesh):
    return jax.shard_map(
        body,
        mesh=mesh,
        in_specs=(P("space", "tm"),),
        out_specs=P(("tm", "space"), None, None),
        check_vma=False,
    )
```

```python
import functools
import math

import jax
import jax.numpy as jnp
from jax import lax
from jax.experimental import pallas as pl
from jax.experimental.pallas import tpu as pltpu
from jax.sharding import PartitionSpec as P

DELAY = 8
PAIRS = 5
CHUNKS = 4
HEAD = 16
SPLIT = 2
LIFT = 2.0 ** (125.0 / 16.0)
MESH = pl.DeviceIdType.MESH
ORDER = [
    (0, 0), (4, 0), 8, (0, 1), ("rows", 0), (1, 0), (0, 2), (3, 0), 9,
    (0, 3), (4, 1), ("cols", 0), 10, ("rows", 1), (1, 1), (3, 1), ("cols", 1), 11,
    (4, 2), 12, ("rows", 2), (1, 2), 13, (3, 2), ("cols", 2), 14, 15,
    ("rows", 3), (2, 0), (2, 1), (2, 2), (4, 3), ("cols", 3), (2, 3), (1, 3), (3, 3),
]
LAG = 4
TASKS = [e for e in ORDER if isinstance(e, tuple) and not isinstance(e[0], str)]
STAGES = 3
STAGE_OF = {}
for _k, _e in enumerate(TASKS):
    STAGE_OF[_k] = -1 if _e[0] in (0, 2) else sum(v >= 0 for v in STAGE_OF.values()) % STAGES


def encode(value):
    top = jnp.max(jnp.abs(value), axis=0, keepdims=True)
    top = jnp.maximum(top, 1e-35).astype(jnp.bfloat16)
    code = value * (LIFT / top.astype(jnp.float32))
    for _ in range(4):
        code = code * code
    code = jnp.where(value < 0.0, -code, code).astype(jnp.bfloat16)
    return code, jnp.broadcast_to(top, (HEAD, value.shape[1]))


def decode(code, top):
    code = code.astype(jnp.float32)
    size = jnp.abs(code)
    for _ in range(4):
        size = lax.rsqrt(size)
    size = size * (top.astype(jnp.float32) * (1.0 / LIFT))
    size = jnp.where(code == 0.0, 0.0, size)
    return jnp.where(code < 0.0, -size, size)


def kernel(
    count, scale, x_ref, out_ref,
    buf, at, hb, hx, hn, saved_one, saved_two, held, stage, inbox, zout, zin, rout, rin,
    local_sem, swap_s, swap_r, cross_s, cross_r, plus_s, plus_r, minus_s, minus_r,
    hswap_s, hswap_r, head_s, head_r, core_s, core_r, z_s, z_r, back_s, back_r, out_sem,
):
    cells, width = x_ref.shape
    half = cells // 2
    chunk = width // CHUNKS
    strip = width // 4
    rows = strip + HEAD
    lane = saved_one.shape[-1]
    piece = half // SPLIT

    t = lax.axis_index("tm")
    s = lax.axis_index("space")
    y = lax.rem(t, 4)
    base = t - y
    zh = lax.rem(lax.div(t, 4), 2)
    zlo = lax.div(s, 2)
    core = lax.rem(s, 2)
    flip = (1 - zlo) * 2 + core
    keep = pl.multiple_of(zh * half, half)
    away = pl.multiple_of((1 - zh) * half, half)

    def block(steps):
        return lax.rem(t + steps + count, count)

    def aligned(steps):
        there = block(steps)
        other = lax.rem(lax.div(there, 4), 2)
        return there, lax.select(other == zh, s, flip)

    partner = (t, flip)
    sibling = (t, zlo * 2 + 1 - core)
    above = (base + lax.rem(y + 1, 4), s)
    below = (base + lax.rem(y + 3, 4), s)
    onward = (block(4), flip)
    heads_to = [aligned(-1), aligned(2), aligned(3)]
    home = (block(-1), s)

    barrier = pltpu.get_barrier_semaphore()
    greet = [partner, sibling, above, below, onward, (block(-4), flip)]
    greet += heads_to + [aligned(1), aligned(-2), aligned(-3)]
    greet += [home, (block(1), s)]
    for device in greet:
        pl.semaphore_signal(barrier, inc=1, device_id=device, device_id_type=MESH)
    pl.semaphore_wait(barrier, len(greet))

    def remote(src, dst, send, recv, device):
        return pltpu.make_async_remote_copy(
            src_ref=src, dst_ref=dst, send_sem=send, recv_sem=recv,
            device_id=device, device_id_type=MESH,
        )

    def local(n):
        q = CHUNKS - 1 - n
        return pltpu.make_async_copy(
            x_ref.at[pl.ds(keep, half), q * chunk : (q + 1) * chunk],
            buf.at[0, q, pl.ds(keep, half), :],
            local_sem.at[n],
        )

    def swap(n, i):
        q = CHUNKS - 1 - n
        off = pl.multiple_of(away + i * piece, piece)
        return remote(
            x_ref.at[pl.ds(off, piece), q * chunk : (q + 1) * chunk],
            buf.at[0, q, pl.ds(off, piece), :],
            swap_s.at[n, i], swap_r.at[n, i], partner,
        )

    def stream(n, phase, source, target, off, send, recv, device):
        q = CHUNKS - 1 - n
        return remote(
            buf.at[source, q, pl.ds(off, piece), :],
            buf.at[target, q, pl.ds(off, piece), :],
            send.at[n, phase], recv.at[n, phase], device,
        )

    def part(first, second, phase):
        start = first if phase < SPLIT else second
        return pl.multiple_of(start + phase % SPLIT * piece, piece)

    def cross(n, phase):
        off = part(keep, away, phase)
        return stream(n, phase, 0, 3, off, cross_s, cross_r, onward)

    def plus(n, phase, source, off):
        return stream(n, phase, source, 1, off, plus_s, plus_r, above)

    def minus(n, phase, source, off):
        return stream(n, phase, source, 2, off, minus_s, minus_r, below)

    def own_ready(n, phase):
        off = part(keep, away, phase)
        cross(n, phase).start()

        @pl.when(y < 3)
        def _():
            plus(n, phase, 0, off).start()

        @pl.when(y == 0)
        def _():
            minus(n, phase, 0, off).start()

    def cross_ready(index):
        n, phase = index // (2 * SPLIT), index % (2 * SPLIT)
        off = part(away, keep, phase)
        cross(n, phase).wait_recv()

        @pl.when(y == 3)
        def _():
            plus(n, phase, 3, off).start()

        @pl.when(y > 0)
        def _():
            minus(n, phase, 3, off).start()

    def transpose(which, source, n):
        q = CHUNKS - 1 - n

        @pl.loop(0, cells // strip)
        def _(i):
            at_cell = pl.multiple_of(i * strip, strip)
            at[which, q * chunk : (q + 1) * chunk, pl.ds(at_cell, strip)] = buf[
                source, q, pl.ds(at_cell, strip), :
            ].T

    head_copy = pltpu.make_async_copy(x_ref.at[:, 0:lane], hx, local_sem.at[CHUNKS])
    head_copy.start()
    for n in range(CHUNKS):
        local(n).start()
    for i in range(SPLIT):
        swap(0, i).start()

    local(0).wait()
    for phase in range(SPLIT):
        own_ready(0, phase)

    head_copy.wait()

    @pl.loop(0, cells // strip)
    def _(i):
        at_cell = pl.multiple_of(i * strip, strip)
        top = hx[pl.ds(at_cell, strip), :].T[0:HEAD]
        hn[:, pl.ds(at_cell, strip)] = jnp.where(t == 0, jnp.zeros_like(top), top)

    hb[1, :, pl.ds(keep, half)] = hn[:, pl.ds(keep, half)]
    head_swap = remote(
        hn.at[:, pl.ds(away, half)], hb.at[1, :, pl.ds(away, half)],
        hswap_s, hswap_r, partner,
    )
    head_swap.start()
    for n in range(1, CHUNKS):
        for i in range(SPLIT):
            swap(n, i).start()
    heads = [
        remote(hb.at[1], hb.at[slot], head_s.at[i], head_r.at[i], device)
        for i, (slot, device) in enumerate(zip((0, 2, 3), heads_to))
    ]

    def strips_of(r, p, q, first, saved, put):
        left = 1 if r == 2 else 0
        right = (0, 1, 2, 2, 3)[r]
        reach = saved.shape[1]
        deep = reach + HEAD - DELAY
        lhs = at[left, pl.ds(pl.multiple_of(p * strip, strip), deep), :]
        gram = jnp.dot(lhs, buf[right, q], preferred_element_type=jnp.float32)
        place = lax.broadcasted_iota(jnp.int32, (reach, lane), 1)
        cols = [gram[0:reach, i : i + lane] for i in range(0, chunk, lane)]
        if first:
            after = lax.dot_general(
                lhs, hb[right], (((1,), (1,)), ((), ())),
                preferred_element_type=jnp.float32,
            )
            after = jnp.concatenate(
                [after, jnp.zeros((deep, lane - HEAD), jnp.float32)], axis=1
            )[0:reach]

        def shifted(value, by):
            return pltpu.roll(pltpu.roll(value, reach - by, 0), lane - by, 1)

        for step, by in enumerate((1, 2, 4)):
            moved = [shifted(col, by) for col in cols]
            if first:
                last = shifted(after, by)
                after = after + last
            else:
                last = saved[step]
            saved[step] = moved[0]
            inside = place < lane - by
            cols = [
                col + jnp.where(inside, here, following)
                for col, here, following in zip(cols, moved, moved[1:] + [last])
            ]
        for i, col in enumerate(cols):
            for j in range((reach - DELAY) // strip):
                put(p + j, i * lane, col[j * strip : (j + 1) * strip] * scale)

    def held_strip(r, p, q, first):
        def put(p, at_lane, value):
            held[q, lax.rem(p, 2), lax.div(p, 2), :, at_lane : at_lane + lane] = value

        strips_of(r, p, q, first, saved_one.at[r // 2, p], put)

    def rows_of(r, n):
        p = CHUNKS - 1 - n
        if n > 0:
            held_strip(r, p, CHUNKS - 1, True)
        if n > 1:

            @pl.loop(1, n)
            def _(m):
                held_strip(r, p, CHUNKS - 1 - m, False)

    def cols_of(r, n):
        @pl.loop(CHUNKS - 1 - n, CHUNKS)
        def _(p):
            held_strip(r, p, CHUNKS - 1 - n, n == 0)

    def source(k):
        r, n = TASKS[k]
        return held.at[CHUNKS - 1 - n] if r in (0, 2) else stage.at[STAGE_OF[k]]

    def core_copy(k):
        return remote(
            source(k).at[1 - core], inbox.at[k], core_s.at[k], core_r.at[k], sibling
        )

    def compute(k):
        r, n = TASKS[k]
        if r not in (0, 2):
            slot = STAGE_OF[k]
            for j in range(k - 1, -1, -1):
                if STAGE_OF[j] == slot:
                    core_copy(j).wait_send()
                    break

            @pl.loop(0, 2)
            def _(pair):
                def put(p, at_lane, value):
                    stage[
                        slot, lax.rem(p, 2), lax.div(p, 2), :, at_lane : at_lane + lane
                    ] = value

                strips_of(
                    r, pair * 2, CHUNKS - 1 - n, n == 0,
                    saved_two.at[(None, 0, None, 1, 2)[r], pair], put,
                )

        core_copy(k).start()

    for n in range(CHUNKS):
        for i in range(SPLIT):
            swap(n, i).wait_recv()
            own_ready(n, SPLIT + i)
        if n + 1 < CHUNKS:
            local(n + 1).wait()
            for phase in range(SPLIT):
                own_ready(n + 1, phase)
        if n == 0:
            head_swap.wait_recv()
            for copy in heads:
                copy.start()
            at[1, width : width + HEAD, :] = hb[1]
        transpose(0, 0, n)
        for i in range(SPLIT):
            cross_ready(n * SPLIT + i)
        if n == 1:
            for copy in heads:
                copy.wait_recv()
            at[0, width : width + HEAD, :] = hb[0]
            rows_of(0, 0)
            cols_of(0, 0)
        if n >= 1:
            rows_of(0, n)
            cols_of(0, n)

    def z_copy(k):
        return remote(zout.at[k], zin.at[k], z_s.at[k], z_r.at[k], partner)

    def back_copy(n):
        return remote(rout.at[n], rin.at[n], back_s.at[n], back_r.at[n], home)

    def out_copy(k):
        r, n = TASKS[k]
        q = CHUNKS - 1 - n
        return pltpu.make_async_copy(
            inbox.at[k, zlo], out_ref.at[r, :, q * chunk : (q + 1) * chunk], out_sem.at[k]
        )

    def send_z(k):
        core_copy(k).wait_recv()
        own = source(k)
        inbox[k, zlo] = own[core, zlo] + inbox[k, zlo]
        code, top = encode(own[core, 1 - zlo] + inbox[k, 1 - zlo])
        zout[k, 0:strip] = code
        zout[k, strip:rows] = top
        z_copy(k).start()

    def finish(k):
        r, n = TASKS[k]
        z_copy(k).wait_recv()
        total = inbox[k, zlo] + decode(zin[k, 0:strip], zin[k, strip : strip + 1])
        if r == 2:
            code, top = encode(total)
            rout[n, 0:strip] = code
            rout[n, strip:rows] = top
            back_copy(n).start()
        else:
            inbox[k, zlo] = total
            out_copy(k).start()

    def block_ready(n, kind):
        for phase in range(2 * SPLIT):
            kind(n, phase, 0, keep).wait_recv()

    k = 0
    for entry in ORDER:
        if not isinstance(entry, tuple):
            cross_ready(entry)
            continue
        r, n = entry
        if r == "rows":
            block_ready(n, plus)
            transpose(1, 1, n)
            rows_of(2, n)
            continue
        if r == "cols":
            if n == 0:
                for j in range(k):
                    if TASKS[j][0] == 0:
                        core_copy(j).wait_send()
            if n == CHUNKS - 1:
                block_ready(n, minus)
            cols_of(2, n)
            continue
        if r == 3 and n < CHUNKS - 1:
            block_ready(n, minus)
        compute(k)
        if k >= 1:
            send_z(k - 1)
        if k >= LAG:
            finish(k - LAG)
        k += 1
    send_z(k - 1)
    for j in range(k - LAG, k):
        finish(j)
    for j, (r, n) in enumerate(TASKS):
        if r == 2:
            back_copy(n).wait_recv()
            inbox[j, zlo] = decode(rin[n, 0:strip], rin[n, strip : strip + 1])
            out_copy(j).start()

    for n in range(CHUNKS):
        for i in range(SPLIT):
            swap(n, i).wait_send()
        back_copy(n).wait_send()
        for phase in range(2 * SPLIT):
            cross(n, phase).wait_send()
            plus(n, phase, 0, keep).wait_send()
            minus(n, phase, 0, keep).wait_send()
    head_swap.wait_send()
    for copy in heads:
        copy.wait_send()
    for slot in range(STAGES):
        core_copy(max(j for j in range(k) if STAGE_OF[j] == slot)).wait_send()
    for j in range(k):
        if TASKS[j][0] == 2:
            core_copy(j).wait_send()
        z_copy(j).wait_send()
        out_copy(j).wait()


def body(snapshots):
    cells, width = snapshots.shape
    count = lax.axis_size("tm")
    scale = 1.0 / math.sqrt(DELAY * cells * lax.axis_size("space"))
    strip, chunk, half = width // 4, width // CHUNKS, cells // 2
    rows = strip + HEAD
    lane = 128
    tasks = len(TASKS)
    dma = pltpu.SemaphoreType.DMA
    f32, bf16 = jnp.float32, jnp.bfloat16
    out = pl.pallas_call(
        functools.partial(kernel, count, scale),
        out_shape=jax.ShapeDtypeStruct((PAIRS, strip, width), f32),
        in_specs=[pl.BlockSpec(memory_space=pl.ANY)],
        out_specs=pl.BlockSpec(memory_space=pl.ANY),
        scratch_shapes=[
            pltpu.VMEM((4, CHUNKS, cells, chunk), bf16),
            pltpu.VMEM((2, width + HEAD, cells), bf16),
            pltpu.VMEM((4, HEAD, cells), bf16),
            pltpu.VMEM((cells, lane), bf16),
            pltpu.VMEM((HEAD, cells), bf16),
            pltpu.VMEM((2, 4, 3, strip + DELAY, lane), f32),
            pltpu.VMEM((3, 2, 3, 2 * strip + DELAY, lane), f32),
            pltpu.VMEM((CHUNKS, 2, 2, strip, chunk), f32),
            pltpu.VMEM((STAGES, 2, 2, strip, chunk), f32),
            pltpu.VMEM((tasks, 2, strip, chunk), f32),
            pltpu.VMEM((tasks, rows, chunk), bf16),
            pltpu.VMEM((tasks, rows, chunk), bf16),
            pltpu.VMEM((CHUNKS, rows, chunk), bf16),
            pltpu.VMEM((CHUNKS, rows, chunk), bf16),
            dma((CHUNKS + 1,)),
            dma((CHUNKS, SPLIT)), dma((CHUNKS, SPLIT)),
            dma((CHUNKS, 2 * SPLIT)), dma((CHUNKS, 2 * SPLIT)),
            dma((CHUNKS, 2 * SPLIT)), dma((CHUNKS, 2 * SPLIT)),
            dma((CHUNKS, 2 * SPLIT)), dma((CHUNKS, 2 * SPLIT)),
            dma, dma,
            dma((3,)), dma((3,)),
            dma((tasks,)), dma((tasks,)),
            dma((tasks,)), dma((tasks,)),
            dma((CHUNKS,)), dma((CHUNKS,)),
            dma((tasks,)),
        ],
        compiler_params=pltpu.CompilerParams(
            collective_id=0, has_side_effects=True, vmem_limit_bytes=60 * 2**20
        ),
        cost_estimate=pl.CostEstimate(
            flops=2 * PAIRS * width * width * cells,
            bytes_accessed=2 * cells * width + 4 * PAIRS * strip * width,
            transcendentals=0,
        ),
    )(snapshots)
    return jnp.transpose(out, (1, 0, 2))


def solution(mesh):
    return jax.shard_map(
        body,
        mesh=mesh,
        in_specs=(P("space", "tm"),),
        out_specs=P(("tm", "space"), None, None),
        check_vma=False,
    )
```

```python
import functools
import math

import jax
import jax.numpy as jnp
from jax import lax
from jax.experimental import pallas as pl
from jax.experimental.pallas import tpu as pltpu
from jax.sharding import PartitionSpec as P

DELAY = 8
PAIRS = 5
CHUNKS = 4
HEAD = 16
SPLIT = 2
LIFT = 2.0 ** (125.0 / 16.0)
MESH = pl.DeviceIdType.MESH
ORDER = [
    (0, 0), (4, 0), 8, (0, 1), ("rows", 0), (1, 0), (0, 2), (3, 0), 9,
    (0, 3), (4, 1), ("cols", 0), 10, ("rows", 1), (1, 1), (3, 1), ("cols", 1), 11,
    (4, 2), 12, ("rows", 2), (1, 2), 13, (3, 2), ("cols", 2), 14, 15,
    (4, 3), ("rows", 3), (2, 0), (2, 1), (2, 2), ("cols", 3), (2, 3), (1, 3), (3, 3),
]
LAG = 4
TASKS = [e for e in ORDER if isinstance(e, tuple) and not isinstance(e[0], str)]
STAGES = 3
STAGE_OF = {}
for _k, _e in enumerate(TASKS):
    STAGE_OF[_k] = -1 if _e[0] in (0, 2) else sum(v >= 0 for v in STAGE_OF.values()) % STAGES


def encode(value):
    top = jnp.max(jnp.abs(value), axis=0, keepdims=True)
    top = jnp.maximum(top, 1e-35).astype(jnp.bfloat16)
    code = value * (LIFT / top.astype(jnp.float32))
    for _ in range(4):
        code = code * code
    code = jnp.where(value < 0.0, -code, code).astype(jnp.bfloat16)
    return code, jnp.broadcast_to(top, (HEAD, value.shape[1]))


def decode(code, top):
    code = code.astype(jnp.float32)
    size = jnp.abs(code)
    for _ in range(4):
        size = lax.rsqrt(size)
    size = size * (top.astype(jnp.float32) * (1.0 / LIFT))
    size = jnp.where(code == 0.0, 0.0, size)
    return jnp.where(code < 0.0, -size, size)


def kernel(
    count, scale, x_ref, out_ref,
    buf, at, hb, hx, hn, saved_one, saved_two, held, stage, inbox, zout, zin, rout, rin,
    local_sem, swap_s, swap_r, cross_s, cross_r, plus_s, plus_r, minus_s, minus_r,
    hswap_s, hswap_r, head_s, head_r, core_s, core_r, z_s, z_r, back_s, back_r, out_sem,
):
    cells, width = x_ref.shape
    half = cells // 2
    chunk = width // CHUNKS
    strip = width // 4
    rows = strip + HEAD
    lane = saved_one.shape[-1]
    piece = half // SPLIT

    t = lax.axis_index("tm")
    s = lax.axis_index("space")
    y = lax.rem(t, 4)
    base = t - y
    zh = lax.rem(lax.div(t, 4), 2)
    zlo = lax.div(s, 2)
    core = lax.rem(s, 2)
    flip = (1 - zlo) * 2 + core
    keep = pl.multiple_of(zh * half, half)
    away = pl.multiple_of((1 - zh) * half, half)

    def block(steps):
        return lax.rem(t + steps + count, count)

    def aligned(steps):
        there = block(steps)
        other = lax.rem(lax.div(there, 4), 2)
        return there, lax.select(other == zh, s, flip)

    partner = (t, flip)
    sibling = (t, zlo * 2 + 1 - core)
    above = (base + lax.rem(y + 1, 4), s)
    below = (base + lax.rem(y + 3, 4), s)
    onward = (block(4), flip)
    heads_to = [aligned(-1), aligned(2), aligned(3)]
    home = (block(-1), s)

    barrier = pltpu.get_barrier_semaphore()
    greet = [partner, sibling, above, below, onward, (block(-4), flip)]
    greet += heads_to + [aligned(1), aligned(-2), aligned(-3)]
    greet += [home, (block(1), s)]
    for device in greet:
        pl.semaphore_signal(barrier, inc=1, device_id=device, device_id_type=MESH)
    pl.semaphore_wait(barrier, len(greet))

    def remote(src, dst, send, recv, device):
        return pltpu.make_async_remote_copy(
            src_ref=src, dst_ref=dst, send_sem=send, recv_sem=recv,
            device_id=device, device_id_type=MESH,
        )

    def local(n):
        q = CHUNKS - 1 - n
        return pltpu.make_async_copy(
            x_ref.at[pl.ds(keep, half), q * chunk : (q + 1) * chunk],
            buf.at[0, q, pl.ds(keep, half), :],
            local_sem.at[n],
        )

    def swap(n, i):
        q = CHUNKS - 1 - n
        off = pl.multiple_of(away + i * piece, piece)
        return remote(
            x_ref.at[pl.ds(off, piece), q * chunk : (q + 1) * chunk],
            buf.at[0, q, pl.ds(off, piece), :],
            swap_s.at[n, i], swap_r.at[n, i], partner,
        )

    def stream(n, phase, source, target, off, send, recv, device):
        q = CHUNKS - 1 - n
        return remote(
            buf.at[source, q, pl.ds(off, piece), :],
            buf.at[target, q, pl.ds(off, piece), :],
            send.at[n, phase], recv.at[n, phase], device,
        )

    def part(first, second, phase):
        start = first if phase < SPLIT else second
        return pl.multiple_of(start + phase % SPLIT * piece, piece)

    def cross(n, phase):
        off = part(keep, away, phase)
        return stream(n, phase, 0, 3, off, cross_s, cross_r, onward)

    def plus(n, phase, source, off):
        return stream(n, phase, source, 1, off, plus_s, plus_r, above)

    def minus(n, phase, source, off):
        return stream(n, phase, source, 2, off, minus_s, minus_r, below)

    def own_ready(n, phase):
        off = part(keep, away, phase)
        cross(n, phase).start()

        @pl.when(y < 3)
        def _():
            plus(n, phase, 0, off).start()

        @pl.when(y == 0)
        def _():
            minus(n, phase, 0, off).start()

    def cross_ready(index):
        n, phase = index // (2 * SPLIT), index % (2 * SPLIT)
        off = part(away, keep, phase)
        cross(n, phase).wait_recv()

        @pl.when(y == 3)
        def _():
            plus(n, phase, 3, off).start()

        @pl.when(y > 0)
        def _():
            minus(n, phase, 3, off).start()

    def transpose(which, source, n):
        q = CHUNKS - 1 - n

        @pl.loop(0, cells // strip)
        def _(i):
            at_cell = pl.multiple_of(i * strip, strip)
            at[which, q * chunk : (q + 1) * chunk, pl.ds(at_cell, strip)] = buf[
                source, q, pl.ds(at_cell, strip), :
            ].T

    head_copy = pltpu.make_async_copy(x_ref.at[:, 0:lane], hx, local_sem.at[CHUNKS])
    head_copy.start()
    for n in range(CHUNKS):
        local(n).start()
    for i in range(SPLIT):
        swap(0, i).start()

    local(0).wait()
    for phase in range(SPLIT):
        own_ready(0, phase)

    head_copy.wait()

    @pl.loop(0, cells // strip)
    def _(i):
        at_cell = pl.multiple_of(i * strip, strip)
        top = hx[pl.ds(at_cell, strip), :].T[0:HEAD]
        hn[:, pl.ds(at_cell, strip)] = jnp.where(t == 0, jnp.zeros_like(top), top)

    hb[1, :, pl.ds(keep, half)] = hn[:, pl.ds(keep, half)]
    head_swap = remote(
        hn.at[:, pl.ds(away, half)], hb.at[1, :, pl.ds(away, half)],
        hswap_s, hswap_r, partner,
    )
    head_swap.start()
    for n in range(1, CHUNKS):
        for i in range(SPLIT):
            swap(n, i).start()
    heads = [
        remote(hb.at[1], hb.at[slot], head_s.at[i], head_r.at[i], device)
        for i, (slot, device) in enumerate(zip((0, 2, 3), heads_to))
    ]

    def strips_of(r, p, q, first, saved, put):
        left = 1 if r == 2 else 0
        right = (0, 1, 2, 2, 3)[r]
        reach = saved.shape[1]
        deep = reach + HEAD - DELAY
        lhs = at[left, pl.ds(pl.multiple_of(p * strip, strip), deep), :]
        gram = jnp.dot(lhs, buf[right, q], preferred_element_type=jnp.float32)
        place = lax.broadcasted_iota(jnp.int32, (reach, lane), 1)
        cols = [gram[0:reach, i : i + lane] for i in range(0, chunk, lane)]
        if first:
            after = lax.dot_general(
                lhs, hb[right], (((1,), (1,)), ((), ())),
                preferred_element_type=jnp.float32,
            )
            after = jnp.concatenate(
                [after, jnp.zeros((deep, lane - HEAD), jnp.float32)], axis=1
            )[0:reach]

        def shifted(value, by):
            return pltpu.roll(pltpu.roll(value, reach - by, 0), lane - by, 1)

        for step, by in enumerate((1, 2, 4)):
            moved = [shifted(col, by) for col in cols]
            if first:
                last = shifted(after, by)
                after = after + last
            else:
                last = saved[step]
            saved[step] = moved[0]
            inside = place < lane - by
            cols = [
                col + jnp.where(inside, here, following)
                for col, here, following in zip(cols, moved, moved[1:] + [last])
            ]
        for i, col in enumerate(cols):
            for j in range((reach - DELAY) // strip):
                put(p + j, i * lane, col[j * strip : (j + 1) * strip] * scale)

    def held_strip(r, p, q, first):
        def put(p, at_lane, value):
            held[q, lax.rem(p, 2), lax.div(p, 2), :, at_lane : at_lane + lane] = value

        strips_of(r, p, q, first, saved_one.at[r // 2, p], put)

    def rows_of(r, n):
        p = CHUNKS - 1 - n
        if n > 0:
            held_strip(r, p, CHUNKS - 1, True)
        if n > 1:

            @pl.loop(1, n)
            def _(m):
                held_strip(r, p, CHUNKS - 1 - m, False)

    def cols_of(r, n):
        @pl.loop(CHUNKS - 1 - n, CHUNKS)
        def _(p):
            held_strip(r, p, CHUNKS - 1 - n, n == 0)

    def source(k):
        r, n = TASKS[k]
        return held.at[CHUNKS - 1 - n] if r in (0, 2) else stage.at[STAGE_OF[k]]

    def core_copy(k):
        return remote(
            source(k).at[1 - core], inbox.at[k], core_s.at[k], core_r.at[k], sibling
        )

    def compute(k):
        r, n = TASKS[k]
        if r not in (0, 2):
            slot = STAGE_OF[k]
            for j in range(k - 1, -1, -1):
                if STAGE_OF[j] == slot:
                    core_copy(j).wait_send()
                    break

            @pl.loop(0, 2)
            def _(pair):
                def put(p, at_lane, value):
                    stage[
                        slot, lax.rem(p, 2), lax.div(p, 2), :, at_lane : at_lane + lane
                    ] = value

                strips_of(
                    r, pair * 2, CHUNKS - 1 - n, n == 0,
                    saved_two.at[(None, 0, None, 1, 2)[r], pair], put,
                )

        core_copy(k).start()

    for n in range(CHUNKS):
        for i in range(SPLIT):
            swap(n, i).wait_recv()
            own_ready(n, SPLIT + i)
        if n + 1 < CHUNKS:
            local(n + 1).wait()
            for phase in range(SPLIT):
                own_ready(n + 1, phase)
        if n == 0:
            head_swap.wait_recv()
            for copy in heads:
                copy.start()
            at[1, width : width + HEAD, :] = hb[1]
        transpose(0, 0, n)
        for i in range(SPLIT):
            cross_ready(n * SPLIT + i)
        if n == 1:
            for copy in heads:
                copy.wait_recv()
            at[0, width : width + HEAD, :] = hb[0]
            rows_of(0, 0)
            cols_of(0, 0)
        if n >= 1:
            rows_of(0, n)
            cols_of(0, n)

    def z_copy(k):
        return remote(zout.at[k], zin.at[k], z_s.at[k], z_r.at[k], partner)

    def back_copy(n):
        return remote(rout.at[n], rin.at[n], back_s.at[n], back_r.at[n], home)

    def out_copy(k):
        r, n = TASKS[k]
        q = CHUNKS - 1 - n
        return pltpu.make_async_copy(
            inbox.at[k, zlo], out_ref.at[r, :, q * chunk : (q + 1) * chunk], out_sem.at[k]
        )

    def send_z(k):
        core_copy(k).wait_recv()
        own = source(k)
        inbox[k, zlo] = own[core, zlo] + inbox[k, zlo]
        code, top = encode(own[core, 1 - zlo] + inbox[k, 1 - zlo])
        zout[k, 0:strip] = code
        zout[k, strip:rows] = top
        z_copy(k).start()

    def finish(k):
        r, n = TASKS[k]
        z_copy(k).wait_recv()
        total = inbox[k, zlo] + decode(zin[k, 0:strip], zin[k, strip : strip + 1])
        if r == 2:
            code, top = encode(total)
            rout[n, 0:strip] = code
            rout[n, strip:rows] = top
            back_copy(n).start()
        else:
            inbox[k, zlo] = total
            out_copy(k).start()

    def block_ready(n, kind):
        for phase in range(2 * SPLIT):
            kind(n, phase, 0, keep).wait_recv()

    k = 0
    for entry in ORDER:
        if not isinstance(entry, tuple):
            cross_ready(entry)
            continue
        r, n = entry
        if r == "rows":
            block_ready(n, plus)
            transpose(1, 1, n)
            rows_of(2, n)
            continue
        if r == "cols":
            if n == 0:
                for j in range(k):
                    if TASKS[j][0] == 0:
                        core_copy(j).wait_send()
            if n == CHUNKS - 1:
                block_ready(n, minus)
            cols_of(2, n)
            continue
        if r == 3 and n < CHUNKS - 1:
            block_ready(n, minus)
        compute(k)
        if k >= 1:
            send_z(k - 1)
        if k >= LAG:
            finish(k - LAG)
        k += 1
    send_z(k - 1)
    for j in range(k - LAG, k):
        finish(j)
    for j, (r, n) in enumerate(TASKS):
        if r == 2:
            back_copy(n).wait_recv()
            inbox[j, zlo] = decode(rin[n, 0:strip], rin[n, strip : strip + 1])
            out_copy(j).start()

    for n in range(CHUNKS):
        for i in range(SPLIT):
            swap(n, i).wait_send()
        back_copy(n).wait_send()
        for phase in range(2 * SPLIT):
            cross(n, phase).wait_send()
            plus(n, phase, 0, keep).wait_send()
            minus(n, phase, 0, keep).wait_send()
    head_swap.wait_send()
    for copy in heads:
        copy.wait_send()
    for slot in range(STAGES):
        core_copy(max(j for j in range(k) if STAGE_OF[j] == slot)).wait_send()
    for j in range(k):
        if TASKS[j][0] == 2:
            core_copy(j).wait_send()
        z_copy(j).wait_send()
        out_copy(j).wait()


def body(snapshots):
    cells, width = snapshots.shape
    count = lax.axis_size("tm")
    scale = 1.0 / math.sqrt(DELAY * cells * lax.axis_size("space"))
    strip, chunk, half = width // 4, width // CHUNKS, cells // 2
    rows = strip + HEAD
    lane = 128
    tasks = len(TASKS)
    dma = pltpu.SemaphoreType.DMA
    f32, bf16 = jnp.float32, jnp.bfloat16
    out = pl.pallas_call(
        functools.partial(kernel, count, scale),
        out_shape=jax.ShapeDtypeStruct((PAIRS, strip, width), f32),
        in_specs=[pl.BlockSpec(memory_space=pl.ANY)],
        out_specs=pl.BlockSpec(memory_space=pl.ANY),
        scratch_shapes=[
            pltpu.VMEM((4, CHUNKS, cells, chunk), bf16),
            pltpu.VMEM((2, width + HEAD, cells), bf16),
            pltpu.VMEM((4, HEAD, cells), bf16),
            pltpu.VMEM((cells, lane), bf16),
            pltpu.VMEM((HEAD, cells), bf16),
            pltpu.VMEM((2, 4, 3, strip + DELAY, lane), f32),
            pltpu.VMEM((3, 2, 3, 2 * strip + DELAY, lane), f32),
            pltpu.VMEM((CHUNKS, 2, 2, strip, chunk), f32),
            pltpu.VMEM((STAGES, 2, 2, strip, chunk), f32),
            pltpu.VMEM((tasks, 2, strip, chunk), f32),
            pltpu.VMEM((tasks, rows, chunk), bf16),
            pltpu.VMEM((tasks, rows, chunk), bf16),
            pltpu.VMEM((CHUNKS, rows, chunk), bf16),
            pltpu.VMEM((CHUNKS, rows, chunk), bf16),
            dma((CHUNKS + 1,)),
            dma((CHUNKS, SPLIT)), dma((CHUNKS, SPLIT)),
            dma((CHUNKS, 2 * SPLIT)), dma((CHUNKS, 2 * SPLIT)),
            dma((CHUNKS, 2 * SPLIT)), dma((CHUNKS, 2 * SPLIT)),
            dma((CHUNKS, 2 * SPLIT)), dma((CHUNKS, 2 * SPLIT)),
            dma, dma,
            dma((3,)), dma((3,)),
            dma((tasks,)), dma((tasks,)),
            dma((tasks,)), dma((tasks,)),
            dma((CHUNKS,)), dma((CHUNKS,)),
            dma((tasks,)),
        ],
        compiler_params=pltpu.CompilerParams(
            collective_id=0, has_side_effects=True, vmem_limit_bytes=60 * 2**20
        ),
        cost_estimate=pl.CostEstimate(
            flops=2 * PAIRS * width * width * cells,
            bytes_accessed=2 * cells * width + 4 * PAIRS * strip * width,
            transcendentals=0,
        ),
    )(snapshots)
    return jnp.transpose(out, (1, 0, 2))


def solution(mesh):
    return jax.shard_map(
        body,
        mesh=mesh,
        in_specs=(P("space", "tm"),),
        out_specs=P(("tm", "space"), None, None),
        check_vma=False,
    )
```
